32 devices in a mesh: tile: 2 (over x), gr: 4 (over y, core), gc: 4 (over z).
Axes of the slice: x: 2, y: 2, z: 4, core: 2. Of those that a mesh axis runs over, the one named last changes fastest.
Arguments:
- child_maps: float32 [2, 8, 1024, 1024], P('tile', None, 'gr', 'gc'), may hold values from -1.3 to 5
Outputs:
- merged: float32 [2, 8, 768, 1536], P('tile', None, 'gr', 'gc')
The draws below stay inside these ranges and needn't reach their ends.
All inputs are finite; a program needn't handle non-finite values.
Results may differ from the reference program's by a relative error of at most 0.0001.
Values sent between devices are 32-bit elements; how exact they have to be, the bound alone decides.
A program may use at most 128 MiB of HBM per device.

```python
import math
import jax
import jax.numpy as jnp
from jax import lax

IFACE = 256
EXTERIOR = 768
MERGES = 8
NEWTON = 4
ORDER = 1024
TILES = 2


def draw_child_maps(key, part):
    map_order = IFACE + EXTERIOR
    key_off, key_diag = jax.random.split(key, 2)
    full_shape = (TILES, MERGES, map_order, map_order)
    offset = jnp.arange(map_order) % (map_order // 4)
    on_iface = offset >= EXTERIOR // 4
    both_iface = on_iface[:, None] & on_iface[None, :]
    one_iface = on_iface[:, None] != on_iface[None, :]
    spread = jnp.where(both_iface, 0.1, jnp.where(one_iface, 0.5, 0.3)) * math.sqrt(3.0)
    base = jax.random.uniform(key_off, full_shape, jnp.float32, -1.0, 1.0)
    diagonal = jnp.exp(jax.random.uniform(key_diag, (TILES, MERGES, map_order), jnp.float32, math.log(2.0), math.log(5.0)))
    eye_mask = jnp.eye(map_order, dtype=bool)
    return jnp.where(eye_mask, diagonal[..., None], base * spread)


def setup_inputs(seed: int = 0) -> dict:
    key_list = jax.random.split(jax.random.key(seed), 2)
    child_maps = draw_child_maps(jax.random.fold_in(key_list[1], 71), 0)
    return {"child_maps": child_maps}


def product(left, right):
    return jnp.matmul(left, right, precision=lax.Precision.HIGHEST)


def split_map(child):
    block_size = ORDER // 4
    ext_count = EXTERIOR // 4
    grid_view = child.reshape(MERGES, 4, block_size, 4, block_size)
    ext_ext = grid_view[:, :, :ext_count, :, :ext_count].reshape(MERGES, EXTERIOR, EXTERIOR)
    ext_int = grid_view[:, :, :ext_count, :, ext_count:].reshape(MERGES, EXTERIOR, IFACE)
    int_ext = grid_view[:, :, ext_count:, :, :ext_count].reshape(MERGES, IFACE, EXTERIOR)
    int_int = grid_view[:, :, ext_count:, :, ext_count:].reshape(MERGES, IFACE, IFACE)
    return ext_ext, ext_int, int_ext, int_int


def alternate(left_part, right_part, leading):
    ext_count = EXTERIOR // 4
    stacked = jnp.stack([left_part.reshape(MERGES, leading, 4, ext_count), right_part.reshape(MERGES, leading, 4, ext_count)], axis=3)
    return stacked.reshape(MERGES, leading, 2 * EXTERIOR)


def merge_pair(pair):
    ee_left, ei_left, ie_left, ii_left = split_map(pair[0])
    ee_right, ei_right, ie_right, ii_right = split_map(pair[1])
    interface = ii_left + ii_right
    largest = jnp.max(jnp.diagonal(interface, axis1=1, axis2=2), axis=1)
    inverse = jnp.eye(IFACE, dtype=jnp.float32)[None] / largest[:, None, None]
    for newton_step in range(NEWTON):
        inverse = 2.0 * inverse - product(product(inverse, interface), inverse)
    solved = alternate(product(inverse, ie_left), product(inverse, ie_right), IFACE)
    blank_part = jnp.zeros_like(ee_left)
    out_left = alternate(ee_left, blank_part, EXTERIOR) - product(ei_left, solved)
    out_right = alternate(blank_part, ee_right, EXTERIOR) - product(ei_right, solved)
    return jnp.stack([out_left, out_right])


def reference(child_maps):
    pairs = child_maps.reshape(TILES // 2, 2, MERGES, ORDER, ORDER)
    result = lax.map(merge_pair, pairs)
    return result.reshape(TILES, MERGES, EXTERIOR, 2 * EXTERIOR)
```

```python
import functools

import jax
import jax.numpy as jnp
from jax import lax
from jax.experimental import pallas as pl
from jax.experimental.pallas import tpu as pltpu
from jax.sharding import PartitionSpec as P

EXTERIOR = 768
NEWTON = 4
MESH = pl.DeviceIdType.MESH
CHUNKS = 4


def dot32(left, right):
    return jnp.dot(
        left, right, precision=lax.Precision.HIGHEST, preferred_element_type=jnp.float32
    )


def halves(x):
    high = x.astype(jnp.bfloat16)
    return high, (x - high.astype(jnp.float32)).astype(jnp.bfloat16)


def dot3(left, right):
    lh, ll = halves(left)
    rh, rl = halves(right)
    dot = functools.partial(jnp.dot, preferred_element_type=jnp.float32)
    return dot(lh, rh) + (dot(lh, rl) + dot(ll, rh))


def kernel(
    groups, x_ref, out_ref, rows, strips, ei, wall,
    row_send, row_recv, strip_send, strip_recv, ei_send, ei_recv, w_send, w_recv,
):
    merges, block, _ = x_ref.shape
    ext = EXTERIOR // 4
    num = block - ext
    half_ext = ext // 2
    per = merges // CHUNKS
    tile = lax.axis_index("tile")
    gr = lax.axis_index("gr")
    gc = lax.axis_index("gc")
    side = tile % 2
    core = gr % 2
    pos = gr // 2
    me = side * 4 + gr

    def across(j):
        far_side = 1 - side if j & 4 else side
        far_pos = 1 - pos if j & 2 else pos
        far_core = 1 - core if j & 1 else core
        device = {"tile": tile - side + far_side, "gr": far_pos * 2 + far_core}
        return device, far_side * 4 + far_pos * 2 + far_core

    barrier = pltpu.get_barrier_semaphore()
    for j in range(1, 8):
        pl.semaphore_signal(barrier, inc=1, device_id=across(j)[0], device_id_type=MESH)
    for d in range(1, groups):
        pl.semaphore_signal(
            barrier, inc=1, device_id={"gc": (gc + d) % groups}, device_id_type=MESH
        )
    pl.semaphore_wait(barrier, 7 + groups - 1)

    def row_copy(part, j):
        device, other = across(j)
        lanes = pl.ds(ext - num, 2 * num) if part == 0 else pl.ds(0, ext - num)
        return pltpu.make_async_remote_copy(
            src_ref=x_ref.at[other, pl.ds(ext, num), lanes],
            dst_ref=rows.at[part, me],
            send_sem=row_send.at[part, j - 1],
            recv_sem=row_recv.at[part, j - 1],
            device_id=device,
            device_id_type=MESH,
        )

    def ei_copy(way, d, k):
        source = gc - d if way == 0 else gc + d
        part = pl.ds(k * per, per)
        return pltpu.make_async_remote_copy(
            src_ref=ei.at[source, part],
            dst_ref=ei.at[source, part],
            send_sem=ei_send.at[way, d, k],
            recv_sem=ei_recv.at[way, d, k],
            device_id={"gc": gc + 1 if way == 0 else gc - 1},
            device_id_type=MESH,
        )

    def sends(way, d):
        if way == 0:
            return jnp.logical_and(gc < groups - 1, gc >= d)
        return jnp.logical_and(gc > 0, gc + d < groups)

    def gets(way, d):
        return gc - 1 - d >= 0 if way == 0 else gc + 1 + d < groups

    def ei_start(d, k):
        for way in range(2):
            @pl.when(sends(way, d))
            def _():
                ei_copy(way, d, k).start()

    def ei_get(d, k):
        for way in range(2):
            @pl.when(gets(way, d))
            def _():
                ei_copy(way, d, k).wait_recv()

    for j in range(1, 8):
        row_copy(0, j).start()
    rows[0, me] = x_ref[me, ext:, ext - num:]
    rows[1, me] = x_ref[me, ext:, : ext - num]

    def pack(m, carry):
        ei[gc, m] = jnp.concatenate(
            [x_ref[m, :half_ext, ext:], x_ref[m, half_ext:ext, ext:]], axis=1
        )
        return carry

    lax.fori_loop(0, merges, pack, 0)
    ei_start(0, 0)
    for j in range(1, 8):
        row_copy(1, j).start()

    for j in range(1, 8):
        row_copy(0, j).wait_recv()
    total = [rows[0, g][:, num:] + rows[0, 4 + g][:, num:] for g in range(4)]
    left = jnp.concatenate(total[:2], axis=0)
    right = jnp.concatenate(total[2:], axis=0)
    strips[gc] = jnp.concatenate([left, right], axis=1)

    def strip_copy(d):
        return pltpu.make_async_remote_copy(
            src_ref=strips.at[gc],
            dst_ref=strips.at[gc],
            send_sem=strip_send.at[d - 1],
            recv_sem=strip_recv.at[d - 1],
            device_id={"gc": (gc + d) % groups},
            device_id_type=MESH,
        )

    for d in range(1, groups):
        strip_copy(d).start()
    for k in range(1, CHUNKS):
        ei_start(0, k)

    for j in range(1, 8):
        row_copy(1, j).wait_recv()
    couplings = jnp.concatenate(
        [
            jnp.concatenate(
                [
                    jnp.concatenate([rows[1, s * 4 + g], rows[0, s * 4 + g][:, :num]], axis=1)
                    for s in range(2)
                ],
                axis=1,
            )
            for g in range(4)
        ],
        axis=0,
    )

    for d in range(1, groups):
        strip_copy(d).wait_recv()
    interface = jnp.concatenate(
        [
            jnp.concatenate([strips[g][:, :num] for g in range(groups)], axis=1),
            jnp.concatenate([strips[g][:, num:] for g in range(groups)], axis=1),
        ],
        axis=0,
    )
    eye = lax.broadcasted_iota(jnp.int32, interface.shape, 0) == lax.broadcasted_iota(
        jnp.int32, interface.shape, 1
    )
    largest = jnp.max(jnp.where(eye, interface, -jnp.inf), axis=(0, 1), keepdims=True)
    scale = 1.0 / largest
    inverse = jnp.where(eye, 2.0 * scale, 0.0) - (interface * scale) * scale
    for step in range(NEWTON - 1):
        inverse = 2.0 * inverse - dot32(dot32(inverse, interface), inverse)
        if step == NEWTON - 3:
            ei_get(0, 0)
            ei_start(1, 0)
    wall[me] = dot32(inverse, couplings)

    size = wall.shape[1] // 2

    def w_copy(index, owner, half, j):
        part = pl.ds(half * size, size)
        return pltpu.make_async_remote_copy(
            src_ref=wall.at[owner, part],
            dst_ref=wall.at[owner, part],
            send_sem=w_send.at[index],
            recv_sem=w_recv.at[index],
            device_id=across(j)[0],
            device_id_type=MESH,
        )

    own = me
    far = {j: across(j)[1] for j in (2, 4, 6)}
    moves = {}
    index = 0
    for half in range(2):
        for j in (4, 2, 1):
            moves["own", half, j] = w_copy(index, own, half, j)
            index += 1
        for j in (4, 2, 6):
            moves["pass", half, j] = w_copy(index, far[j], half, 1)
            index += 1
    moves["turn", 1, 4] = w_copy(index, far[4], 1, 2)
    moves["turn", 0, 2] = w_copy(index + 1, far[2], 0, 4)

    for half in (1, 0):
        for j in (4, 2) if half else (2, 4):
            moves["own", half, j].start()
    for half in (1, 0):
        moves["own", half, 1].start()
    for k in range(1, CHUNKS):
        ei_get(0, k)
        ei_start(1, k)
    moves["own", 1, 4].wait_recv()
    moves["turn", 1, 4].start()
    moves["pass", 1, 4].start()
    moves["own", 0, 2].wait_recv()
    moves["turn", 0, 2].start()
    moves["pass", 0, 2].start()
    for d in range(1, groups - 1):
        for k in range(CHUNKS):
            ei_get(d, k)
            if d + 1 < groups - 1:
                ei_start(d + 1, k)
        if d == 1:
            for half, j in ((1, 2), (0, 4)):
                moves["own", half, j].wait_recv()
                moves["pass", half, j].start()
            moves["turn", 1, 4].wait_recv()
            moves["pass", 1, 6].start()
            moves["turn", 0, 2].wait_recv()
            moves["pass", 0, 6].start()
    for half in range(2):
        moves["own", half, 1].wait_recv()
        for j in (4, 2, 6):
            moves["pass", half, j].wait_recv()

    def finish(m, carry):
        coupling = jnp.concatenate(
            [
                jnp.concatenate([ei[g, m][:, :num] for g in range(groups)], axis=1),
                jnp.concatenate([ei[g, m][:, num:] for g in range(groups)], axis=1),
            ],
            axis=0,
        )
        own_part = x_ref[m, :ext, :ext]
        blank = jnp.zeros_like(own_part)
        first = jnp.where(side == 0, own_part, blank)
        second = jnp.where(side == 0, blank, own_part)
        out_ref[m] = jnp.concatenate([first, second], axis=1) - dot3(coupling, wall[m])
        return carry

    lax.fori_loop(0, merges, finish, 0)

    for j in range(1, 8):
        for part in range(2):
            row_copy(part, j).wait_send()
    for d in range(1, groups):
        strip_copy(d).wait_send()
    for way in range(2):
        for d in range(groups - 1):
            @pl.when(sends(way, d))
            def _():
                for k in range(CHUNKS):
                    ei_copy(way, d, k).wait_send()
    for move in moves.values():
        move.wait_send()


def on_device(groups, child_maps):
    blocks = child_maps[0]
    merges, block, _ = blocks.shape
    ext = EXTERIOR // 4
    num = block - ext
    dma = pltpu.SemaphoreType.DMA
    f32 = jnp.float32
    merged = pl.pallas_call(
        functools.partial(kernel, groups),
        out_shape=jax.ShapeDtypeStruct((merges, ext, 2 * ext), f32),
        in_specs=[pl.BlockSpec(memory_space=pltpu.VMEM)],
        out_specs=pl.BlockSpec(memory_space=pltpu.VMEM),
        scratch_shapes=[
            pltpu.VMEM((2, merges, num, 2 * num), f32),
            pltpu.VMEM((groups, 2 * num, 2 * num), f32),
            pltpu.VMEM((groups, merges, ext // 2, 2 * num), f32),
            pltpu.VMEM((merges, 4 * num, 2 * ext), f32),
            dma((2, 7)),
            dma((2, 7)),
            dma((groups - 1,)),
            dma((groups - 1,)),
            dma((2, groups - 1, CHUNKS)),
            dma((2, groups - 1, CHUNKS)),
            dma((14,)),
            dma((14,)),
        ],
        compiler_params=pltpu.CompilerParams(
            collective_id=0, has_side_effects=True, vmem_limit_bytes=48 * 1024 * 1024
        ),
    )(blocks)
    return merged[None]


def solution(mesh):
    in_specs = (P("tile", None, "gr", "gc"),)
    out_specs = P("tile", None, "gr", "gc")
    return jax.shard_map(
        functools.partial(on_device, mesh.shape["gc"]),
        mesh=mesh, in_specs=in_specs, out_specs=out_specs, check_vma=False,
    )
```

```python
import functools

import jax
import jax.numpy as jnp
from jax import lax
from jax.experimental import pallas as pl
from jax.experimental.pallas import tpu as pltpu
from jax.sharding import PartitionSpec as P

EXTERIOR = 768
NEWTON = 4
MESH = pl.DeviceIdType.MESH
CHUNKS = 4


def dot32(left, right):
    return jnp.dot(
        left, right, precision=lax.Precision.HIGHEST, preferred_element_type=jnp.float32
    )


def halves(x):
    high = x.astype(jnp.bfloat16)
    return high, (x - high.astype(jnp.float32)).astype(jnp.bfloat16)


def dot3(left, right):
    lh, ll = halves(left)
    rh, rl = halves(right)
    dot = functools.partial(jnp.dot, preferred_element_type=jnp.float32)
    return dot(lh, rh) + (dot(lh, rl) + dot(ll, rh))


def kernel(
    groups, hbm_ref, out_ref, x_ref, rows, strips, ei, ie, inv, wall, load,
    row_send, row_recv, strip_send, strip_recv, ei_send, ei_recv,
    ie_send, ie_recv, inv_send, inv_recv,
):
    merges, block, _ = x_ref.shape
    ext = EXTERIOR // 4
    num = block - ext
    half_ext = ext // 2
    half_num = num // 2
    wide = ext - num
    per = merges // CHUNKS
    tile = lax.axis_index("tile")
    gr = lax.axis_index("gr")
    gc = lax.axis_index("gc")
    side = tile % 2
    core = gr % 2
    pos = gr // 2
    me = side * 4 + gr

    staged = pltpu.make_async_copy(hbm_ref, x_ref, load)
    staged.start()

    def across(j):
        far_side = 1 - side if j & 4 else side
        far_pos = 1 - pos if j & 2 else pos
        far_core = 1 - core if j & 1 else core
        device = {"tile": tile - side + far_side, "gr": far_pos * 2 + far_core}
        return device, far_side * 4 + far_pos * 2 + far_core

    barrier = pltpu.get_barrier_semaphore()
    for j in range(1, 8):
        pl.semaphore_signal(barrier, inc=1, device_id=across(j)[0], device_id_type=MESH)
    for d in range(1, groups):
        pl.semaphore_signal(
            barrier, inc=1, device_id={"gc": (gc + d) % groups}, device_id_type=MESH
        )
    pl.semaphore_wait(barrier, 7 + groups - 1)
    staged.wait()

    def row_copy(j):
        device, other = across(j)
        return pltpu.make_async_remote_copy(
            src_ref=x_ref.at[other, pl.ds(ext, num), pl.ds(wide, 2 * num)],
            dst_ref=rows.at[me],
            send_sem=row_send.at[j - 1],
            recv_sem=row_recv.at[j - 1],
            device_id=device,
            device_id_type=MESH,
        )

    def gather_moves(buf, send_sems, recv_sems):
        size = buf.shape[1] // 2

        def move(index, owner, half, j):
            part = pl.ds(half * size, size)
            return pltpu.make_async_remote_copy(
                src_ref=buf.at[owner, part],
                dst_ref=buf.at[owner, part],
                send_sem=send_sems.at[index],
                recv_sem=recv_sems.at[index],
                device_id=across(j)[0],
                device_id_type=MESH,
            )

        far = {j: across(j)[1] for j in (2, 4, 6)}
        moves = {}
        index = 0
        for half in range(2):
            for j in (4, 2, 1):
                moves["own", half, j] = move(index, me, half, j)
                index += 1
            for j in (4, 2, 6):
                moves["pass", half, j] = move(index, far[j], half, 1)
                index += 1
        moves["turn", 1, 4] = move(index, far[4], 1, 2)
        moves["turn", 0, 2] = move(index + 1, far[2], 0, 4)
        return moves

    def send_own(moves):
        for half, j in ((1, 4), (0, 2), (0, 4), (1, 2), (1, 1), (0, 1)):
            moves["own", half, j].start()

    def send_turns(moves):
        for half, j in ((1, 4), (0, 2)):
            moves["own", half, j].wait_recv()
            moves["turn", half, j].start()
            moves["pass", half, j].start()

    def send_rest(moves):
        for half, j in ((0, 4), (1, 2)):
            moves["own", half, j].wait_recv()
            moves["pass", half, j].start()

    def send_diagonal(moves):
        for half, j in ((1, 4), (0, 2)):
            moves["turn", half, j].wait_recv()
            moves["pass", half, 6].start()

    def get_rest(moves):
        for half in range(2):
            moves["own", half, 1].wait_recv()
            for j in (4, 2, 6):
                moves["pass", half, j].wait_recv()

    def ei_copy(way, d, k):
        source = gc - d if way == 0 else gc + d
        part = pl.ds(k * per, per)
        return pltpu.make_async_remote_copy(
            src_ref=ei.at[source, part],
            dst_ref=ei.at[source, part],
            send_sem=ei_send.at[way, d, k],
            recv_sem=ei_recv.at[way, d, k],
            device_id={"gc": gc + 1 if way == 0 else gc - 1},
            device_id_type=MESH,
        )

    def sends(way, d):
        if way == 0:
            return jnp.logical_and(gc < groups - 1, gc >= d)
        return jnp.logical_and(gc > 0, gc + d < groups)

    def gets(way, d):
        return gc - 1 - d >= 0 if way == 0 else gc + 1 + d < groups

    def ei_start(d, k):
        for way in range(2):
            @pl.when(sends(way, d))
            def _():
                ei_copy(way, d, k).start()

    def ei_get(d, k):
        for way in range(2):
            @pl.when(gets(way, d))
            def _():
                ei_copy(way, d, k).wait_recv()

    for j in range(1, 8):
        row_copy(j).start()
    rows[me] = x_ref[me, ext:, wide:]

    def pack_ei(m, carry):
        ei[gc, m] = jnp.concatenate(
            [x_ref[m, :half_ext, ext:], x_ref[m, half_ext:ext, ext:]], axis=1
        )
        return carry

    def pack_ie(m, carry):
        ie[me, m, :num] = x_ref[m, ext:, :wide]
        ie[me, m, num:] = jnp.concatenate(
            [x_ref[m, ext : ext + half_num, wide:ext], x_ref[m, ext + half_num :, wide:ext]],
            axis=1,
        )
        return carry

    lax.fori_loop(0, merges, pack_ei, 0)
    for k in range(CHUNKS // 2):
        ei_start(0, k)
    lax.fori_loop(0, merges, pack_ie, 0)
    ie_moves = gather_moves(ie, ie_send, ie_recv)
    inv_moves = gather_moves(inv, inv_send, inv_recv)
    send_own(ie_moves)

    for j in range(1, 8):
        row_copy(j).wait_recv()
    total = [rows[g][:, num:] + rows[4 + g][:, num:] for g in range(4)]
    left = jnp.concatenate(total[:2], axis=0)
    right = jnp.concatenate(total[2:], axis=0)
    strips[gc] = jnp.concatenate([left, right], axis=1)

    def strip_copy(d):
        return pltpu.make_async_remote_copy(
            src_ref=strips.at[gc],
            dst_ref=strips.at[gc],
            send_sem=strip_send.at[d - 1],
            recv_sem=strip_recv.at[d - 1],
            device_id={"gc": (gc + d) % groups},
            device_id_type=MESH,
        )

    for d in range(1, groups):
        strip_copy(d).start()
    for k in range(CHUNKS // 2, CHUNKS):
        ei_start(0, k)
    for k in range(CHUNKS // 2):
        ei_get(0, k)
        ei_start(1, k)
    send_turns(ie_moves)

    for d in range(1, groups):
        strip_copy(d).wait_recv()
    interface = jnp.concatenate(
        [
            jnp.concatenate([strips[g][:, :num] for g in range(groups)], axis=1),
            jnp.concatenate([strips[g][:, num:] for g in range(groups)], axis=1),
        ],
        axis=0,
    )
    eye = lax.broadcasted_iota(jnp.int32, interface.shape, 0) == lax.broadcasted_iota(
        jnp.int32, interface.shape, 1
    )
    largest = jnp.max(jnp.where(eye, interface, -jnp.inf), axis=(0, 1), keepdims=True)
    scale = 1.0 / largest
    inverse = jnp.where(eye, 2.0 * scale, 0.0) - (interface * scale) * scale
    for step in range(NEWTON - 1):
        inverse = 2.0 * inverse - dot32(dot32(inverse, interface), inverse)
    inv[me] = inverse
    send_own(inv_moves)

    for k in range(CHUNKS // 2, CHUNKS):
        ei_get(0, k)
        ei_start(1, k)
    send_rest(ie_moves)
    send_diagonal(ie_moves)
    for k in range(CHUNKS // 2):
        ei_get(1, k)
        ei_start(2, k)
    send_turns(inv_moves)
    for k in range(CHUNKS // 2, CHUNKS):
        ei_get(1, k)
        ei_start(2, k)
    send_rest(inv_moves)
    send_diagonal(inv_moves)
    get_rest(ie_moves)
    get_rest(inv_moves)

    def solve(m, carry):
        for g in range(4):
            parts = []
            for s in range(2):
                parts.append(ie[s * 4 + g, m, :num])
                parts.append(
                    jnp.concatenate(
                        [ie[s * 4 + g, m, num:, :num], ie[s * 4 + g, m, num:, num:]], axis=0
                    )
                )
            wall[m, pl.ds(g * num, num)] = jnp.concatenate(parts, axis=1)
        wall[m] = dot3(inv[m], wall[m])
        return carry

    lax.fori_loop(0, merges, solve, 0)

    def finish(m, carry):
        coupling = jnp.concatenate(
            [
                jnp.concatenate([ei[g, m][:, :num] for g in range(groups)], axis=1),
                jnp.concatenate([ei[g, m][:, num:] for g in range(groups)], axis=1),
            ],
            axis=0,
        )
        own_part = x_ref[m, :ext, :ext]
        blank = jnp.zeros_like(own_part)
        first = jnp.where(side == 0, own_part, blank)
        second = jnp.where(side == 0, blank, own_part)
        out_ref[m] = jnp.concatenate([first, second], axis=1) - dot3(coupling, wall[m])
        return carry

    for k in range(CHUNKS):
        for d in range(2, groups - 1):
            ei_get(d, k)
        lax.fori_loop(k * per, (k + 1) * per, finish, 0)

    for j in range(1, 8):
        row_copy(j).wait_send()
    for d in range(1, groups):
        strip_copy(d).wait_send()
    for way in range(2):
        for d in range(groups - 1):
            @pl.when(sends(way, d))
            def _():
                for k in range(CHUNKS):
                    ei_copy(way, d, k).wait_send()
    for move in (*ie_moves.values(), *inv_moves.values()):
        move.wait_send()


def on_device(groups, child_maps):
    blocks = child_maps[0]
    merges, block, _ = blocks.shape
    ext = EXTERIOR // 4
    num = block - ext
    dma = pltpu.SemaphoreType.DMA
    f32 = jnp.float32
    merged = pl.pallas_call(
        functools.partial(kernel, groups),
        out_shape=jax.ShapeDtypeStruct((merges, ext, 2 * ext), f32),
        in_specs=[pl.BlockSpec(memory_space=pltpu.HBM)],
        out_specs=pl.BlockSpec(memory_space=pltpu.VMEM),
        scratch_shapes=[
            pltpu.VMEM((merges, block, block), f32),
            pltpu.VMEM((merges, num, 2 * num), f32),
            pltpu.VMEM((groups, 2 * num, 2 * num), f32),
            pltpu.VMEM((groups, merges, ext // 2, 2 * num), f32),
            pltpu.VMEM((merges, merges, num + num // 2, 2 * num), f32),
            pltpu.VMEM((merges, 4 * num, 4 * num), f32),
            pltpu.VMEM((merges, 4 * num, 2 * ext), f32),
            dma,
            dma((7,)),
            dma((7,)),
            dma((groups - 1,)),
            dma((groups - 1,)),
            dma((2, groups - 1, CHUNKS)),
            dma((2, groups - 1, CHUNKS)),
            dma((14,)),
            dma((14,)),
            dma((14,)),
            dma((14,)),
        ],
        compiler_params=pltpu.CompilerParams(
            collective_id=0, has_side_effects=True, vmem_limit_bytes=48 * 1024 * 1024
        ),
    )(blocks)
    return merged[None]


def solution(mesh):
    in_specs = (P("tile", None, "gr", "gc"),)
    out_specs = P("tile", None, "gr", "gc")
    return jax.shard_map(
        functools.partial(on_device, mesh.shape["gc"]),
        mesh=mesh, in_specs=in_specs, out_specs=out_specs, check_vma=False,
    )
```

```python
import functools

import jax
import jax.numpy as jnp
from jax import lax
from jax.experimental import pallas as pl
from jax.experimental.pallas import tpu as pltpu
from jax.sharding import PartitionSpec as P

EXTERIOR = 768
NEWTON = 4
MESH = pl.DeviceIdType.MESH
CHUNKS = 4


def dot32(left, right):
    return jnp.dot(
        left, right, precision=lax.Precision.HIGHEST, preferred_element_type=jnp.float32
    )


def halves(x):
    high = x.astype(jnp.bfloat16)
    return high, (x - high.astype(jnp.float32)).astype(jnp.bfloat16)


def dot3(left, right):
    lh, ll = halves(left)
    rh, rl = halves(right)
    dot = functools.partial(jnp.dot, preferred_element_type=jnp.float32)
    return dot(lh, rh) + (dot(lh, rl) + dot(ll, rh))


def kernel(
    groups, hbm_ref, out_ref, x_ref, ii, rows, strips, ei, ie, inv, wall, load,
    row_send, row_recv, strip_send, strip_recv, ei_send, ei_recv,
    ie_send, ie_recv, inv_send, inv_recv,
):
    merges, block, _ = x_ref.shape
    ext = EXTERIOR // 4
    num = block - ext
    half_ext = ext // 2
    half_num = num // 2
    wide = ext - num
    per = merges // CHUNKS
    tile = lax.axis_index("tile")
    gr = lax.axis_index("gr")
    gc = lax.axis_index("gc")
    side = tile % 2
    core = gr % 2
    pos = gr // 2
    me = side * 4 + gr

    staged = pltpu.make_async_copy(hbm_ref, x_ref, load)
    staged.start()

    def across(j):
        far_side = 1 - side if j & 4 else side
        far_pos = 1 - pos if j & 2 else pos
        far_core = 1 - core if j & 1 else core
        device = {"tile": tile - side + far_side, "gr": far_pos * 2 + far_core}
        return device, far_side * 4 + far_pos * 2 + far_core

    barrier = pltpu.get_barrier_semaphore()
    for j in range(1, 8):
        pl.semaphore_signal(barrier, inc=1, device_id=across(j)[0], device_id_type=MESH)
    for d in range(1, groups):
        pl.semaphore_signal(
            barrier, inc=1, device_id={"gc": (gc + d) % groups}, device_id_type=MESH
        )
    pl.semaphore_wait(barrier, 7 + groups - 1)
    staged.wait()

    def row_copy(j):
        device, other = across(j)
        return pltpu.make_async_remote_copy(
            src_ref=ii.at[other],
            dst_ref=rows.at[me],
            send_sem=row_send.at[j - 1],
            recv_sem=row_recv.at[j - 1],
            device_id=device,
            device_id_type=MESH,
        )

    def gather_moves(buf, send_sems, recv_sems):
        size = buf.shape[1] // 2

        def move(index, owner, half, j):
            part = pl.ds(half * size, size)
            return pltpu.make_async_remote_copy(
                src_ref=buf.at[owner, part],
                dst_ref=buf.at[owner, part],
                send_sem=send_sems.at[index],
                recv_sem=recv_sems.at[index],
                device_id=across(j)[0],
                device_id_type=MESH,
            )

        far = {j: across(j)[1] for j in (2, 4, 6)}
        moves = {}
        index = 0
        for half in range(2):
            for j in (4, 2, 1):
                moves["own", half, j] = move(index, me, half, j)
                index += 1
            for j in (4, 2, 6):
                moves["pass", half, j] = move(index, far[j], half, 1)
                index += 1
        moves["turn", 1, 4] = move(index, far[4], 1, 2)
        moves["turn", 0, 2] = move(index + 1, far[2], 0, 4)
        return moves

    def send_own(moves):
        for half, j in ((1, 4), (0, 2), (0, 4), (1, 2), (1, 1), (0, 1)):
            moves["own", half, j].start()

    def send_turns(moves):
        for half, j in ((1, 4), (0, 2)):
            moves["own", half, j].wait_recv()
            moves["turn", half, j].start()
            moves["pass", half, j].start()

    def send_rest(moves):
        for half, j in ((0, 4), (1, 2)):
            moves["own", half, j].wait_recv()
            moves["pass", half, j].start()

    def send_diagonal(moves):
        for half, j in ((1, 4), (0, 2)):
            moves["turn", half, j].wait_recv()
            moves["pass", half, 6].start()

    def get_rest(moves):
        for half in range(2):
            moves["own", half, 1].wait_recv()
            for j in (4, 2, 6):
                moves["pass", half, j].wait_recv()

    def ei_copy(way, d, k):
        source = gc - d if way == 0 else gc + d
        part = pl.ds(k * per, per)
        return pltpu.make_async_remote_copy(
            src_ref=ei.at[source, part],
            dst_ref=ei.at[source, part],
            send_sem=ei_send.at[way, d, k],
            recv_sem=ei_recv.at[way, d, k],
            device_id={"gc": gc + 1 if way == 0 else gc - 1},
            device_id_type=MESH,
        )

    def sends(way, d):
        if way == 0:
            return jnp.logical_and(gc < groups - 1, gc >= d)
        return jnp.logical_and(gc > 0, gc + d < groups)

    def gets(way, d):
        return gc - 1 - d >= 0 if way == 0 else gc + 1 + d < groups

    def ei_start(d, k):
        for way in range(2):
            @pl.when(sends(way, d))
            def _():
                ei_copy(way, d, k).start()

    def ei_get(d, k):
        for way in range(2):
            @pl.when(gets(way, d))
            def _():
                ei_copy(way, d, k).wait_recv()

    for m in range(merges):
        ii[m] = jnp.concatenate(
            [x_ref[m, ext : ext + half_num, ext:], x_ref[m, ext + half_num :, ext:]], axis=1
        )
    for j in (6, 7, 4, 5, 2, 3, 1):
        row_copy(j).start()
    rows[me] = ii[me]

    def pack_ei(m, carry):
        ei[gc, m] = jnp.concatenate(
            [x_ref[m, :half_ext, ext:], x_ref[m, half_ext:ext, ext:]], axis=1
        )
        return carry

    def pack_ie(m, carry):
        ie[me, m, :num] = x_ref[m, ext:, :wide]
        ie[me, m, num:] = jnp.concatenate(
            [x_ref[m, ext : ext + half_num, wide:ext], x_ref[m, ext + half_num :, wide:ext]],
            axis=1,
        )
        return carry

    lax.fori_loop(0, merges, pack_ei, 0)
    for k in range(CHUNKS // 2):
        ei_start(0, k)
    lax.fori_loop(0, merges, pack_ie, 0)
    ie_moves = gather_moves(ie, ie_send, ie_recv)
    inv_moves = gather_moves(inv, inv_send, inv_recv)
    send_own(ie_moves)

    for j in range(1, 8):
        row_copy(j).wait_recv()
    total = [rows[g] + rows[4 + g] for g in range(4)]
    total = [part for pair in total for part in (pair[:, :num], pair[:, num:])]
    left = jnp.concatenate(total[:4], axis=0)
    right = jnp.concatenate(total[4:], axis=0)
    strips[gc] = jnp.concatenate([left, right], axis=1)

    def strip_copy(d):
        return pltpu.make_async_remote_copy(
            src_ref=strips.at[gc],
            dst_ref=strips.at[gc],
            send_sem=strip_send.at[d - 1],
            recv_sem=strip_recv.at[d - 1],
            device_id={"gc": (gc + d) % groups},
            device_id_type=MESH,
        )

    for d in range(1, groups):
        strip_copy(d).start()
    for k in range(CHUNKS // 2, CHUNKS):
        ei_start(0, k)
    for k in range(CHUNKS // 2):
        ei_get(0, k)
        ei_start(1, k)
    send_turns(ie_moves)

    for d in range(1, groups):
        strip_copy(d).wait_recv()
    interface = jnp.concatenate(
        [
            jnp.concatenate([strips[g][:, :num] for g in range(groups)], axis=1),
            jnp.concatenate([strips[g][:, num:] for g in range(groups)], axis=1),
        ],
        axis=0,
    )
    eye = lax.broadcasted_iota(jnp.int32, interface.shape, 0) == lax.broadcasted_iota(
        jnp.int32, interface.shape, 1
    )
    largest = jnp.max(jnp.where(eye, interface, -jnp.inf), axis=(0, 1), keepdims=True)
    scale = 1.0 / largest
    inverse = jnp.where(eye, 2.0 * scale, 0.0) - (interface * scale) * scale
    for step in range(NEWTON - 1):
        inverse = 2.0 * inverse - dot32(dot32(inverse, interface), inverse)
    inv[me] = inverse
    send_own(inv_moves)

    for k in range(CHUNKS // 2, CHUNKS):
        ei_get(0, k)
        ei_start(1, k)
    send_rest(ie_moves)
    send_diagonal(ie_moves)
    for k in range(CHUNKS // 2):
        ei_get(1, k)
        ei_start(2, k)
    send_turns(inv_moves)
    for k in range(CHUNKS // 2, CHUNKS):
        ei_get(1, k)
        ei_start(2, k)
    send_rest(inv_moves)
    send_diagonal(inv_moves)
    get_rest(ie_moves)
    get_rest(inv_moves)

    def solve(m, carry):
        for g in range(4):
            parts = []
            for s in range(2):
                parts.append(ie[s * 4 + g, m, :num])
                parts.append(
                    jnp.concatenate(
                        [ie[s * 4 + g, m, num:, :num], ie[s * 4 + g, m, num:, num:]], axis=0
                    )
                )
            wall[m, pl.ds(g * num, num)] = jnp.concatenate(parts, axis=1)
        wall[m] = dot3(inv[m], wall[m])
        return carry

    lax.fori_loop(0, merges, solve, 0)

    def finish(m, carry):
        coupling = jnp.concatenate(
            [
                jnp.concatenate([ei[g, m][:, :num] for g in range(groups)], axis=1),
                jnp.concatenate([ei[g, m][:, num:] for g in range(groups)], axis=1),
            ],
            axis=0,
        )
        own_part = x_ref[m, :ext, :ext]
        blank = jnp.zeros_like(own_part)
        first = jnp.where(side == 0, own_part, blank)
        second = jnp.where(side == 0, blank, own_part)
        out_ref[m] = jnp.concatenate([first, second], axis=1) - dot3(coupling, wall[m])
        return carry

    for k in range(CHUNKS):
        for d in range(2, groups - 1):
            ei_get(d, k)
        lax.fori_loop(k * per, (k + 1) * per, finish, 0)

    for j in range(1, 8):
        row_copy(j).wait_send()
    for d in range(1, groups):
        strip_copy(d).wait_send()
    for way in range(2):
        for d in range(groups - 1):
            @pl.when(sends(way, d))
            def _():
                for k in range(CHUNKS):
                    ei_copy(way, d, k).wait_send()
    for move in (*ie_moves.values(), *inv_moves.values()):
        move.wait_send()


def on_device(groups, child_maps):
    blocks = child_maps[0]
    merges, block, _ = blocks.shape
    ext = EXTERIOR // 4
    num = block - ext
    dma = pltpu.SemaphoreType.DMA
    f32 = jnp.float32
    merged = pl.pallas_call(
        functools.partial(kernel, groups),
        out_shape=jax.ShapeDtypeStruct((merges, ext, 2 * ext), f32),
        in_specs=[pl.BlockSpec(memory_space=pltpu.HBM)],
        out_specs=pl.BlockSpec(memory_space=pltpu.VMEM),
        scratch_shapes=[
            pltpu.VMEM((merges, block, block), f32),
            pltpu.VMEM((merges, num // 2, 2 * num), f32),
            pltpu.VMEM((merges, num // 2, 2 * num), f32),
            pltpu.VMEM((groups, 2 * num, 2 * num), f32),
            pltpu.VMEM((groups, merges, ext // 2, 2 * num), f32),
            pltpu.VMEM((merges, merges, num + num // 2, 2 * num), f32),
            pltpu.VMEM((merges, 4 * num, 4 * num), f32),
            pltpu.VMEM((merges, 4 * num, 2 * ext), f32),
            dma,
            dma((7,)),
            dma((7,)),
            dma((groups - 1,)),
            dma((groups - 1,)),
            dma((2, groups - 1, CHUNKS)),
            dma((2, groups - 1, CHUNKS)),
            dma((14,)),
            dma((14,)),
            dma((14,)),
            dma((14,)),
        ],
        compiler_params=pltpu.CompilerParams(
            collective_id=0, has_side_effects=True, vmem_limit_bytes=48 * 1024 * 1024
        ),
    )(blocks)
    return merged[None]


def solution(mesh):
    in_specs = (P("tile", None, "gr", "gc"),)
    out_specs = P("tile", None, "gr", "gc")
    return jax.shard_map(
        functools.partial(on_device, mesh.shape["gc"]),
        mesh=mesh, in_specs=in_specs, out_specs=out_specs, check_vma=False,
    )
```

```python
import functools

import jax
import jax.numpy as jnp
from jax import lax
from jax.experimental import pallas as pl
from jax.experimental.pallas import tpu as pltpu
from jax.sharding import PartitionSpec as P

EXTERIOR = 768
NEWTON = 4
MESH = pl.DeviceIdType.MESH
CHUNKS = 4


def dot32(left, right):
    return jnp.dot(
        left, right, precision=lax.Precision.HIGHEST, preferred_element_type=jnp.float32
    )


def halves(x):
    high = x.astype(jnp.bfloat16)
    return high, (x - high.astype(jnp.float32)).astype(jnp.bfloat16)


def dot3(left, right):
    lh, ll = halves(left)
    rh, rl = halves(right)
    dot = functools.partial(jnp.dot, preferred_element_type=jnp.float32)
    return dot(lh, rh) + (dot(lh, rl) + dot(ll, rh))


def kernel(
    groups, hbm_ref, out_ref, x_ref, ii, rows, strips, ei, ie, inv, wall, load,
    row_send, row_recv, strip_send, strip_recv, ei_send, ei_recv,
    ie_send, ie_recv, inv_send, inv_recv,
):
    merges, block, _ = x_ref.shape
    ext = EXTERIOR // 4
    num = block - ext
    half_ext = ext // 2
    half_num = num // 2
    wide = ext - num
    per = merges // CHUNKS
    tile = lax.axis_index("tile")
    gr = lax.axis_index("gr")
    gc = lax.axis_index("gc")
    side = tile % 2
    core = gr % 2
    pos = gr // 2
    me = side * 4 + gr

    staged = pltpu.make_async_copy(hbm_ref, x_ref, load)
    staged.start()

    def across(j):
        far_side = 1 - side if j & 4 else side
        far_pos = 1 - pos if j & 2 else pos
        far_core = 1 - core if j & 1 else core
        device = {"tile": tile - side + far_side, "gr": far_pos * 2 + far_core}
        return device, far_side * 4 + far_pos * 2 + far_core

    barrier = pltpu.get_barrier_semaphore()
    for j in range(1, 8):
        pl.semaphore_signal(barrier, inc=1, device_id=across(j)[0], device_id_type=MESH)
    for d in range(1, groups):
        pl.semaphore_signal(
            barrier, inc=1, device_id={"gc": (gc + d) % groups}, device_id_type=MESH
        )

    def row_copy(j):
        device, other = across(j)
        return pltpu.make_async_remote_copy(
            src_ref=ii.at[other],
            dst_ref=rows.at[me],
            send_sem=row_send.at[j - 1],
            recv_sem=row_recv.at[j - 1],
            device_id=device,
            device_id_type=MESH,
        )

    def gather_moves(buf, send_sems, recv_sems):
        size = buf.shape[1] // 2

        def move(index, owner, half, j):
            part = pl.ds(half * size, size)
            return pltpu.make_async_remote_copy(
                src_ref=buf.at[owner, part],
                dst_ref=buf.at[owner, part],
                send_sem=send_sems.at[index],
                recv_sem=recv_sems.at[index],
                device_id=across(j)[0],
                device_id_type=MESH,
            )

        far = {j: across(j)[1] for j in (2, 4, 6)}
        moves = {}
        index = 0
        for half in range(2):
            for j in (4, 2, 1):
                moves["own", half, j] = move(index, me, half, j)
                index += 1
            for j in (4, 2, 6):
                moves["pass", half, j] = move(index, far[j], half, 1)
                index += 1
        moves["turn", 1, 4] = move(index, far[4], 1, 2)
        moves["turn", 0, 2] = move(index + 1, far[2], 0, 4)
        return moves

    def send_own(moves):
        for half, j in ((1, 4), (0, 2), (0, 4), (1, 2), (1, 1), (0, 1)):
            moves["own", half, j].start()

    def send_turns(moves):
        for half, j in ((1, 4), (0, 2)):
            moves["own", half, j].wait_recv()
            moves["turn", half, j].start()
            moves["pass", half, j].start()

    def send_rest(moves):
        for half, j in ((0, 4), (1, 2)):
            moves["own", half, j].wait_recv()
            moves["pass", half, j].start()

    def send_diagonal(moves):
        for half, j in ((1, 4), (0, 2)):
            moves["turn", half, j].wait_recv()
            moves["pass", half, 6].start()

    def get_rest(moves):
        for half in range(2):
            moves["own", half, 1].wait_recv()
            for j in (4, 2, 6):
                moves["pass", half, j].wait_recv()

    def ei_copy(way, d, k):
        source = gc - d if way == 0 else gc + d
        part = pl.ds(k * per, per)
        return pltpu.make_async_remote_copy(
            src_ref=ei.at[source, part],
            dst_ref=ei.at[source, part],
            send_sem=ei_send.at[way, d, k],
            recv_sem=ei_recv.at[way, d, k],
            device_id={"gc": gc + 1 if way == 0 else gc - 1},
            device_id_type=MESH,
        )

    def sends(way, d):
        if way == 0:
            return jnp.logical_and(gc < groups - 1, gc >= d)
        return jnp.logical_and(gc > 0, gc + d < groups)

    def gets(way, d):
        return gc - 1 - d >= 0 if way == 0 else gc + 1 + d < groups

    def ei_start(d, k):
        for way in range(2):
            @pl.when(sends(way, d))
            def _():
                ei_copy(way, d, k).start()

    def ei_get(d, k):
        for way in range(2):
            @pl.when(gets(way, d))
            def _():
                ei_copy(way, d, k).wait_recv()

    staged.wait()
    for m in range(merges):
        ii[m] = jnp.concatenate(
            [x_ref[m, ext : ext + half_num, ext:], x_ref[m, ext + half_num :, ext:]], axis=1
        )
    rows[me] = ii[me]

    def pack_ei(m, carry):
        ei[gc, m] = jnp.concatenate(
            [x_ref[m, :half_ext, ext:], x_ref[m, half_ext:ext, ext:]], axis=1
        )
        return carry

    def pack_ie(m, carry):
        ie[me, m, :num] = x_ref[m, ext:, :wide]
        ie[me, m, num:] = jnp.concatenate(
            [x_ref[m, ext : ext + half_num, wide:ext], x_ref[m, ext + half_num :, wide:ext]],
            axis=1,
        )
        return carry

    lax.fori_loop(0, merges, pack_ei, 0)
    lax.fori_loop(0, merges, pack_ie, 0)
    pl.semaphore_wait(barrier, 7 + groups - 1)
    for j in (6, 7, 4, 5, 2, 3, 1):
        row_copy(j).start()
    for k in range(CHUNKS // 2):
        ei_start(0, k)
    ie_moves = gather_moves(ie, ie_send, ie_recv)
    inv_moves = gather_moves(inv, inv_send, inv_recv)
    send_own(ie_moves)

    for j in range(1, 8):
        row_copy(j).wait_recv()
    total = [rows[g] + rows[4 + g] for g in range(4)]
    total = [part for pair in total for part in (pair[:, :num], pair[:, num:])]
    left = jnp.concatenate(total[:4], axis=0)
    right = jnp.concatenate(total[4:], axis=0)
    strips[gc] = jnp.concatenate([left, right], axis=1)

    def strip_copy(d):
        return pltpu.make_async_remote_copy(
            src_ref=strips.at[gc],
            dst_ref=strips.at[gc],
            send_sem=strip_send.at[d - 1],
            recv_sem=strip_recv.at[d - 1],
            device_id={"gc": (gc + d) % groups},
            device_id_type=MESH,
        )

    for d in range(1, groups):
        strip_copy(d).start()
    for k in range(CHUNKS // 2, CHUNKS):
        ei_start(0, k)
    for k in range(CHUNKS // 2):
        ei_get(0, k)
        ei_start(1, k)
    send_turns(ie_moves)

    for d in range(1, groups):
        strip_copy(d).wait_recv()
    interface = jnp.concatenate(
        [
            jnp.concatenate([strips[g][:, :num] for g in range(groups)], axis=1),
            jnp.concatenate([strips[g][:, num:] for g in range(groups)], axis=1),
        ],
        axis=0,
    )
    eye = lax.broadcasted_iota(jnp.int32, interface.shape, 0) == lax.broadcasted_iota(
        jnp.int32, interface.shape, 1
    )
    largest = jnp.max(jnp.where(eye, interface, -jnp.inf), axis=(0, 1), keepdims=True)
    scale = 1.0 / largest
    inverse = jnp.where(eye, 2.0 * scale, 0.0) - (interface * scale) * scale
    for step in range(NEWTON - 1):
        inverse = 2.0 * inverse - dot32(dot32(inverse, interface), inverse)
    inv[me] = inverse
    send_own(inv_moves)

    for k in range(CHUNKS // 2, CHUNKS):
        ei_get(0, k)
        ei_start(1, k)
    send_rest(ie_moves)
    send_diagonal(ie_moves)
    for k in range(CHUNKS // 2):
        ei_get(1, k)
        ei_start(2, k)
    send_turns(inv_moves)
    for k in range(CHUNKS // 2, CHUNKS):
        ei_get(1, k)
        ei_start(2, k)
    send_rest(inv_moves)
    send_diagonal(inv_moves)
    get_rest(ie_moves)
    get_rest(inv_moves)

    def solve(m, carry):
        for g in range(4):
            parts = []
            for s in range(2):
                parts.append(ie[s * 4 + g, m, :num])
                parts.append(
                    jnp.concatenate(
                        [ie[s * 4 + g, m, num:, :num], ie[s * 4 + g, m, num:, num:]], axis=0
                    )
                )
            wall[m, pl.ds(g * num, num)] = jnp.concatenate(parts, axis=1)
        wall[m] = dot3(inv[m], wall[m])
        return carry

    lax.fori_loop(0, merges, solve, 0)

    def finish(m, carry):
        coupling = jnp.concatenate(
            [
                jnp.concatenate([ei[g, m][:, :num] for g in range(groups)], axis=1),
                jnp.concatenate([ei[g, m][:, num:] for g in range(groups)], axis=1),
            ],
            axis=0,
        )
        own_part = x_ref[m, :ext, :ext]
        blank = jnp.zeros_like(own_part)
        first = jnp.where(side == 0, own_part, blank)
        second = jnp.where(side == 0, blank, own_part)
        out_ref[m] = jnp.concatenate([first, second], axis=1) - dot3(coupling, wall[m])
        return carry

    for k in range(CHUNKS):
        for d in range(2, groups - 1):
            ei_get(d, k)
        lax.fori_loop(k * per, (k + 1) * per, finish, 0)

    for j in range(1, 8):
        row_copy(j).wait_send()
    for d in range(1, groups):
        strip_copy(d).wait_send()
    for way in range(2):
        for d in range(groups - 1):
            @pl.when(sends(way, d))
            def _():
                for k in range(CHUNKS):
                    ei_copy(way, d, k).wait_send()
    for move in (*ie_moves.values(), *inv_moves.values()):
        move.wait_send()


def on_device(groups, child_maps):
    blocks = child_maps[0]
    merges, block, _ = blocks.shape
    ext = EXTERIOR // 4
    num = block - ext
    dma = pltpu.SemaphoreType.DMA
    f32 = jnp.float32
    merged = pl.pallas_call(
        functools.partial(kernel, groups),
        out_shape=jax.ShapeDtypeStruct((merges, ext, 2 * ext), f32),
        in_specs=[pl.BlockSpec(memory_space=pltpu.HBM)],
        out_specs=pl.BlockSpec(memory_space=pltpu.VMEM),
        scratch_shapes=[
            pltpu.VMEM((merges, block, block), f32),
            pltpu.VMEM((merges, num // 2, 2 * num), f32),
            pltpu.VMEM((merges, num // 2, 2 * num), f32),
            pltpu.VMEM((groups, 2 * num, 2 * num), f32),
            pltpu.VMEM((groups, merges, ext // 2, 2 * num), f32),
            pltpu.VMEM((merges, merges, num + num // 2, 2 * num), f32),
            pltpu.VMEM((merges, 4 * num, 4 * num), f32),
            pltpu.VMEM((merges, 4 * num, 2 * ext), f32),
            dma,
            dma((7,)),
            dma((7,)),
            dma((groups - 1,)),
            dma((groups - 1,)),
            dma((2, groups - 1, CHUNKS)),
            dma((2, groups - 1, CHUNKS)),
            dma((14,)),
            dma((14,)),
            dma((14,)),
            dma((14,)),
        ],
        compiler_params=pltpu.CompilerParams(
            collective_id=0, has_side_effects=True, vmem_limit_bytes=48 * 1024 * 1024
        ),
    )(blocks)
    return merged[None]


def solution(mesh):
    in_specs = (P("tile", None, "gr", "gc"),)
    out_specs = P("tile", None, "gr", "gc")
    return jax.shard_map(
        functools.partial(on_device, mesh.shape["gc"]),
        mesh=mesh, in_specs=in_specs, out_specs=out_specs, check_vma=False,
    )
```
